512 devices in a mesh: ctx: 64 (over x_hi, z, core), head: 8 (over y, x_lo).
Axes of the slice: x: 4 (x_hi: 2, x_lo: 2; x = x_hi * 2 + x_lo), y: 4, z: 16, core: 2. Of those that a mesh axis runs over, the one named last changes fastest.
Arguments:
- hidden_in: bfloat16 [24576, 6144], P(('ctx', 'head')), may hold values from -6 to 6
- norm_gain: float32 [6144], replicated, may hold values from 0.1 to 1.9
- qkv_weight: bfloat16 [6144, 5120], P('ctx', 'head'), may hold values from -0.15625 to 0.15625
- out_grad: bfloat16 [24576, 3072], P('ctx', 'head'), may hold values from -6 to 6
- doc_ids: int32 [24576], replicated, may hold values from 0 to 63, never falling along the last dimension, each value on 1 to 1536 neighbouring positions
Outputs:
- attn_out: bfloat16 [24576, 3072], P('ctx', 'head')
- qkv_grad: bfloat16 [24576, 5120], P(('ctx', 'head'))
The draws below stay inside these ranges and needn't reach their ends.
Inputs may be any that keep to these rules, and one draw needn't show every extreme that they name: `doc_ids`: ids never fall along the sequence; each document has 1 to 1536 tokens, one exactly 1536.
All inputs are finite; a program needn't handle non-finite values.
Results may differ from the reference program's by a relative error of at most 0.02.
The reference program's roundings to bfloat16 on the way count: a program that leaves them out, or rounds other values in their place, can miss the bound.
Values may be sent and summed in bfloat16 or wider, within the bound.
No kernel may reach another device: no remote copies, remote signals or barrier semaphores. Data moves between devices by JAX's collectives and lax.ppermute only.
A program may use at most 64 MiB of HBM per device.

```python
import math
import jax
import jax.numpy as jnp
import numpy as np
from jax import lax

D = 6144
Q_HEADS = 24
KV_HEADS = 8
HEAD_DIM = 128
GROUP = 3
BLK = 384
SPAN = 768
TOKENS = 24576
N_CTX = 64


def shard_levels(own_key, shape, cuts, low, high):
    factor_of, own = 1.0, jax.random.fold_in(own_key, 6)
    for position, blocks in cuts:
        draws = jnp.exp(jax.random.uniform(jax.random.fold_in(own, position), (blocks,), jnp.float32, low / len(cuts), high / len(cuts)))
        factor_of = factor_of * jnp.repeat(draws, shape[position] // blocks).reshape([-1 if axis == position else 1 for axis in range(len(shape))])
    return factor_of


def split_up(amount, total, most, slope):
    loads = [(1 << 20) // math.isqrt(standing ** slope) + 1 for standing in range(2, amount + 1)]
    spare, counts = total - most - (amount - 1), [1] * (amount - 1)
    while spare > 0:
        free = [i for i in range(amount - 1) if counts[i] < most]
        pool, budget = sum([loads[i] for i in free]), spare
        for i in free:
            extra = min(most - counts[i], max(1, budget * loads[i] // pool), spare)
            counts[i] = counts[i] + extra
            spare = spare - extra
    return np.array([most] + counts)


def ragged(own_key, number_of, total, bound, lean):
    if number_of == 2:
        one = jax.random.randint(own_key, (), max(1, total - bound), min(bound, total - 1) + 1)
        return jnp.stack([one, total - one])
    tallies = jnp.asarray(split_up(number_of, total, bound, lean), jnp.int32)
    twos = (number_of - 1) // 2
    source_of, sink = tallies[1:1 + 2 * twos:2], tallies[2:2 + 2 * twos:2]
    room = jnp.minimum(source_of - 1, bound - sink)
    passed = jax.random.randint(jax.random.fold_in(own_key, 1), (twos,), 0, 1 << 20) % (room + 1)
    tallies = tallies.at[1:1 + 2 * twos:2].set(source_of - passed).at[2:2 + 2 * twos:2].set(sink + passed)
    return tallies[jax.random.permutation(jax.random.fold_in(own_key, 2), number_of)]


def scatter_about(own_key, shape, spread, bound, split=(), held_as=jnp.bfloat16):
    drawn = spread * jax.random.normal(own_key, shape, jnp.float32)
    if split:
        drawn = drawn * shard_levels(own_key, shape, split, -0.22, 0.18)
    return jnp.clip(drawn, -bound, bound).astype(held_as)


def setup_inputs(seed: int = 0) -> dict:
    key_list = jax.random.split(jax.random.key(seed), 6)
    hidden_in = scatter_about(key_list[0], (TOKENS, D), 1.0, 6.0, ((0, 512),))
    norm_gain = jnp.clip(1.0 + 0.18 * jax.random.normal(key_list[1], (D,), jnp.float32), 0.1, 1.9)
    qkv_weight = scatter_about(key_list[2], (D, KV_HEADS * (GROUP + 2) * HEAD_DIM), (D // 4) ** -0.5, 0.15625, ((0, 64), (1, 8)))
    out_grad = scatter_about(key_list[3], (TOKENS, Q_HEADS * HEAD_DIM), 1.0, 6.0, ((0, 64), (1, 8)))
    doc_ids = jnp.searchsorted(jnp.cumsum(ragged(key_list[4], TOKENS // BLK, TOKENS, 4 * BLK, 2)), jnp.arange(TOKENS), side="right").astype(jnp.int32)
    return {"hidden_in": hidden_in, "norm_gain": norm_gain, "qkv_weight": qkv_weight, "out_grad": out_grad, "doc_ids": doc_ids}


def norm_rows(hidden_in, norm_gain):
    values = hidden_in.astype(jnp.float32)
    mean_sq = lax.optimization_barrier(jnp.mean(values * values, axis=-1, keepdims=True))
    return (values * lax.rsqrt(mean_sq + 1e-06) * norm_gain).astype(jnp.bfloat16)

def attend_block(query, keys, values, grad_out, allowed):
    scale = HEAD_DIM ** (-0.5)
    query_f = query.astype(jnp.float32)
    keys_f = keys.astype(jnp.float32)
    values_f = values.astype(jnp.float32)
    grad_f = grad_out.astype(jnp.float32)
    scores = jnp.einsum('rgd,kd->grk', query_f, keys_f) * scale
    scores = jnp.where(allowed[None], scores, jnp.float32(-1e+30))
    expo = jnp.exp(scores)
    total = lax.optimization_barrier(jnp.sum(expo, axis=-1, keepdims=True))
    prob = expo / total
    prob_b = prob.astype(jnp.bfloat16)
    prob_bf = prob_b.astype(jnp.float32)
    out_b = jnp.einsum('grk,kd->rgd', prob_bf, values_f).astype(jnp.bfloat16)
    delta = lax.optimization_barrier(jnp.sum(grad_f * out_b.astype(jnp.float32), axis=-1))
    delta = jnp.transpose(delta)[:, :, None]
    dprob = jnp.einsum('rgd,kd->grk', grad_f, values_f)
    dscore = (prob * (dprob - delta)).astype(jnp.bfloat16).astype(jnp.float32)
    grad_q = jnp.einsum('grk,kd->rgd', dscore, keys_f) * scale
    grad_k = jnp.einsum('grk,rgd->kd', dscore, query_f) * scale
    grad_v = jnp.einsum('grk,rgd->kd', prob_bf, grad_f)
    return (out_b, grad_q, grad_k, grad_v)

def reference(hidden_in, norm_gain, qkv_weight, out_grad, doc_ids):
    width = (GROUP + 2) * HEAD_DIM
    normed = norm_rows(hidden_in, norm_gain)
    qkv = jnp.dot(normed, qkv_weight, preferred_element_type=jnp.float32).astype(jnp.bfloat16)
    qkv = qkv.reshape(TOKENS, KV_HEADS, width)
    query = qkv[:, :, :GROUP * HEAD_DIM].reshape(TOKENS, KV_HEADS, GROUP, HEAD_DIM)
    keys = qkv[:, :, GROUP * HEAD_DIM:(GROUP + 1) * HEAD_DIM]
    values = qkv[:, :, (GROUP + 1) * HEAD_DIM:]
    grads = out_grad.reshape(TOKENS, KV_HEADS, GROUP, HEAD_DIM)
    front = jnp.zeros((2 * BLK, KV_HEADS, HEAD_DIM), jnp.bfloat16)
    keys_pad = jnp.concatenate([front, keys], axis=0)
    values_pad = jnp.concatenate([front, values], axis=0)
    docs_pad = jnp.concatenate([jnp.full((2 * BLK,), -1, jnp.int32), doc_ids.astype(jnp.int32)])
    gap = (jnp.arange(BLK, dtype=jnp.int32) + 2 * BLK)[:, None] - jnp.arange(3 * BLK, dtype=jnp.int32)[None, :]

    def one_block(index):
        start = (index * BLK).astype(jnp.int32)
        block_q = lax.dynamic_slice_in_dim(query, start, BLK, 0)
        block_g = lax.dynamic_slice_in_dim(grads, start, BLK, 0)
        block_k = lax.dynamic_slice_in_dim(keys_pad, start, 3 * BLK, 0)
        block_v = lax.dynamic_slice_in_dim(values_pad, start, 3 * BLK, 0)
        query_docs = lax.dynamic_slice_in_dim(doc_ids.astype(jnp.int32), start, BLK, 0)
        key_docs = lax.dynamic_slice_in_dim(docs_pad, start, 3 * BLK, 0)
        allowed = (gap >= 0) & (gap < SPAN) & (query_docs[:, None] == key_docs[None, :])
        return jax.vmap(attend_block, in_axes=(1, 1, 1, 1, None), out_axes=1)(block_q, block_k, block_v, block_g, allowed)
    outs, grad_q, grad_k, grad_v = lax.map(one_block, jnp.arange(N_CTX, dtype=jnp.int32))
    attn_out = outs.reshape(TOKENS, Q_HEADS * HEAD_DIM)
    pieces = jnp.stack([grad_k, grad_v], axis=1).reshape(N_CTX, 2, 3, BLK, KV_HEADS, HEAD_DIM)
    zero_one = jnp.zeros((1, 2, BLK, KV_HEADS, HEAD_DIM), jnp.float32)
    zero_two = jnp.zeros((2, 2, BLK, KV_HEADS, HEAD_DIM), jnp.float32)
    summed = pieces[:, :, 2] + jnp.concatenate([pieces[1:, :, 1], zero_one], axis=0)
    summed = summed + jnp.concatenate([pieces[2:, :, 0], zero_two], axis=0)
    summed = summed.astype(jnp.bfloat16)
    grad_kt = summed[:, 0].reshape(TOKENS, KV_HEADS, HEAD_DIM)
    grad_vt = summed[:, 1].reshape(TOKENS, KV_HEADS, HEAD_DIM)
    grad_qt = grad_q.astype(jnp.bfloat16).reshape(TOKENS, KV_HEADS, GROUP * HEAD_DIM)
    qkv_grad = jnp.concatenate([grad_qt, grad_kt, grad_vt], axis=-1).reshape(TOKENS, KV_HEADS * width)
    return (attn_out, qkv_grad)
```

```python
import functools

import jax
import jax.numpy as jnp
from jax import lax
from jax.experimental import pallas as pl
from jax.experimental.pallas import tpu as pltpu
from jax.sharding import Mesh
from jax.sharding import PartitionSpec as P

HEAD_DIM = 128
GROUP = 3
CTX = ("x_hi", "z", "core")
HEAD = ("y", "x_lo")
SIZES = {"x_hi": 2, "z": 16, "core": 2, "y": 4, "x_lo": 2}


def turned(value, axis, steps):
    count = SIZES[axis]
    return lax.ppermute(value, axis, [(i, (i + steps) % count) for i in range(count)])


def passed_along(value, steps):
    count = 64
    first, last = (max(0, -steps), min(count, count - steps))
    return lax.ppermute(value, CTX, [(i, i + steps) for i in range(first, last)])


def norm_rows(hidden_in, norm_gain):
    values = hidden_in.astype(jnp.float32)
    mean_sq = jnp.mean(values * values, axis=-1, keepdims=True)
    return (values * lax.rsqrt(mean_sq + 1e-06) * norm_gain).astype(jnp.bfloat16)


def gather_weight(own):
    rows = own.shape[0]
    from_m4 = turned(own, "z", 4)
    from_p4 = turned(own, "z", -4)
    from_p8 = turned(own, "z", 8)
    near = jnp.concatenate([from_p4, own, from_m4, from_p8], axis=0)
    at = [4, 0, -4, 8]
    far = turned(near, "x_hi", 1)

    def spread(part, flag):
        from_m1 = turned(part, "z", 1)
        from_p1 = turned(part, "z", -1)
        from_m2 = turned(part[rows : 3 * rows], "z", 2)
        from_p2 = turned(part[: 2 * rows], "z", -2)
        joined = jnp.concatenate([from_m1, from_p1, from_m2, from_p2], axis=0)
        chunks = [b - 1 for b in at] + [b + 1 for b in at] + [b - 2 for b in at[1:3]] + [b + 2 for b in at[:2]]
        return (joined, [(flag, b, 0) for b in chunks])

    pieces = [
        (jnp.concatenate([near, far], axis=0), [(0, b, 0) for b in at] + [(1, b, 0) for b in at]),
        spread(near, 0),
        spread(far, 1),
    ]
    for array, chunks in list(pieces):
        pieces.append((turned(array, "core", 1), [(a, b, 1) for a, b, _ in chunks]))
    return pieces


def project_body(chunk_lists, token_lists, step, *refs):
    n_w, n_t = len(chunk_lists), len(token_lists)
    weights = refs[:n_w]
    tokens = refs[n_w : n_w + n_t]
    q_ref, kv_ref = refs[n_w + n_t : n_w + n_t + 2]
    full, rows, total, sem = refs[n_w + n_t + 2 :]
    x_hi, z, core = (lax.axis_index(name) for name in CTX)
    y, x_lo = (lax.axis_index(name) for name in HEAD)
    copies = []
    for ref, chunks in zip(weights, chunk_lists):
        size = ref.shape[0] // len(chunks)
        for j, (a, b, c) in enumerate(chunks):
            slot = ((x_hi + a) % 2) * 32 + ((z + b + 16) % 16) * 2 + (core + c) % 2
            target = full.at[pl.ds(pl.multiple_of(slot * size, 16), size)]
            copies.append((ref.at[pl.ds(j * size, size)], target))
    for ref, blocks in zip(tokens, token_lists):
        size = ref.shape[0] // len(blocks)
        for j, (relative, a, b) in enumerate(blocks):
            slot = ((y + a + 4) % 4 if relative else a) * 2 + (x_lo + b) % 2
            target = rows.at[pl.ds(pl.multiple_of(slot * size, 16), size)]
            copies.append((ref.at[pl.ds(j * size, size)], target))
    copies = [pltpu.make_async_copy(s, d, sem.at[i]) for i, (s, d) in enumerate(copies)]
    for copy in copies:
        copy.start()
    for copy in copies:
        copy.wait()
    total[...] = jnp.zeros_like(total)

    @pl.loop(0, full.shape[0] // step)
    def _(k):
        at = pl.ds(pl.multiple_of(k * step, step), step)
        total[...] += jnp.dot(rows[:, at], full[at, :], preferred_element_type=jnp.float32)

    split = GROUP * HEAD_DIM
    q_ref[...] = total[:, :split].astype(q_ref.dtype)
    kv_ref[0] = total[:, split : split + HEAD_DIM].astype(kv_ref.dtype)
    kv_ref[1] = total[:, split + HEAD_DIM :].astype(kv_ref.dtype)


def project(pieces, tokens):
    columns = pieces[0][0].shape[1]
    depth = tokens[0][0].shape[1]
    n_rows = sum(array.shape[0] for array, _ in tokens)
    n_copies = sum(len(chunks) for _, chunks in pieces) + sum(len(blocks) for _, blocks in tokens)
    arrays = [array for array, _ in pieces] + [array for array, _ in tokens]
    body = functools.partial(
        project_body, [chunks for _, chunks in pieces], [blocks for _, blocks in tokens], 768
    )
    return pl.pallas_call(
        body,
        out_shape=(
            jax.ShapeDtypeStruct((n_rows, GROUP * HEAD_DIM), jnp.bfloat16),
            jax.ShapeDtypeStruct((2, n_rows, HEAD_DIM), jnp.bfloat16),
        ),
        in_specs=[pl.BlockSpec(memory_space=pl.ANY)] * len(arrays),
        out_specs=(pl.BlockSpec(memory_space=pltpu.VMEM), pl.BlockSpec(memory_space=pltpu.VMEM)),
        scratch_shapes=[
            pltpu.VMEM((depth, columns), jnp.bfloat16),
            pltpu.VMEM((n_rows, depth), jnp.bfloat16),
            pltpu.VMEM((n_rows, columns), jnp.float32),
            pltpu.SemaphoreType.DMA((n_copies,)),
        ],
        compiler_params=pltpu.CompilerParams(vmem_limit_bytes=24 * 1024 * 1024),
        cost_estimate=pl.CostEstimate(
            flops=2 * n_rows * depth * columns, bytes_accessed=2 * depth * (columns + n_rows), transcendentals=0
        ),
        name="project",
    )(*arrays)


def attend_block(query, keys, values, grad_out, allowed):
    scale = query.shape[-1] ** (-0.5)
    scores = jnp.einsum("rgd,kd->grk", query, keys, preferred_element_type=jnp.float32) * scale
    scores = jnp.where(allowed[None], scores, jnp.float32(-1e30))
    expo = jnp.exp(scores)
    total = jnp.sum(expo, axis=-1, keepdims=True)
    prob = expo / total
    prob_b = prob.astype(jnp.bfloat16)
    out_b = jnp.einsum("grk,kd->rgd", prob_b, values, preferred_element_type=jnp.float32).astype(
        jnp.bfloat16
    )
    delta = jnp.sum(grad_out.astype(jnp.float32) * out_b.astype(jnp.float32), axis=-1)
    delta = jnp.transpose(delta)[:, :, None]
    dprob = jnp.einsum("rgd,kd->grk", grad_out, values, preferred_element_type=jnp.float32)
    dscore = (prob * (dprob - delta)).astype(jnp.bfloat16)
    grad_q = jnp.einsum("grk,kd->rgd", dscore, keys, preferred_element_type=jnp.float32) * scale
    grad_k = jnp.einsum("grk,rgd->kd", dscore, query, preferred_element_type=jnp.float32) * scale
    grad_v = jnp.einsum("grk,rgd->kd", prob_b, grad_out, preferred_element_type=jnp.float32)
    return (out_b, grad_q, grad_k, grad_v)


def per_device(hidden_in, norm_gain, qkv_weight, out_grad, doc_ids):
    pieces = gather_weight(qkv_weight)
    own = norm_rows(hidden_in, norm_gain)
    other = turned(own, "x_lo", 1)
    tokens = [
        (lax.all_gather(own, "y", axis=0, tiled=True), [(False, a, 0) for a in range(4)]),
        (lax.all_gather(other, "y", axis=0, tiled=True), [(False, a, 1) for a in range(4)]),
    ]
    return finish(pieces, tokens, out_grad, doc_ids)


def finish(pieces, tokens, out_grad, doc_ids):
    rows = out_grad.shape[0]
    query, own_kv = project(pieces, tokens)
    near_kv = passed_along(own_kv, 1)
    far_kv = passed_along(own_kv, 2)
    window_kv = jnp.concatenate([far_kv, near_kv, own_kv], axis=1)
    block = lax.axis_index(CTX)
    start = block * rows
    padded_docs = jnp.concatenate([jnp.full((2 * rows,), -1, jnp.int32), doc_ids])
    query_docs = lax.dynamic_slice_in_dim(doc_ids, start, rows, 0)
    key_docs = lax.dynamic_slice_in_dim(padded_docs, start, 3 * rows, 0)
    gap = (jnp.arange(rows, dtype=jnp.int32) + 2 * rows)[:, None] - jnp.arange(
        3 * rows, dtype=jnp.int32
    )[None, :]
    allowed = (gap >= 0) & (gap < 2 * rows) & (query_docs[:, None] == key_docs[None, :])
    outs, grad_q, grad_k, grad_v = attend_block(
        query.reshape(rows, GROUP, HEAD_DIM),
        window_kv[0],
        window_kv[1],
        out_grad.reshape(rows, GROUP, HEAD_DIM),
        allowed,
    )
    kv_terms = jnp.stack([grad_k, grad_v])
    from_near = passed_along(kv_terms[:, rows : 2 * rows].astype(jnp.bfloat16), -1)
    from_far = passed_along(kv_terms[:, :rows].astype(jnp.bfloat16), -2)
    kv_total = kv_terms[:, 2 * rows :] + from_near.astype(jnp.float32) + from_far.astype(jnp.float32)
    kv_total = kv_total.astype(jnp.bfloat16)
    grad_qt = grad_q.astype(jnp.bfloat16).reshape(rows, GROUP * HEAD_DIM)
    block_grad = jnp.concatenate([grad_qt, kv_total[0], kv_total[1]], axis=-1)
    qkv_grad = lax.all_to_all(block_grad, HEAD, split_axis=0, concat_axis=1, tiled=True)
    return (outs.reshape(rows, GROUP * HEAD_DIM), qkv_grad)


def solution(mesh):
    fine = Mesh(mesh.devices.reshape(tuple(SIZES.values())), tuple(SIZES))
    in_specs = (P((*CTX, *HEAD), None), P(), P(CTX, HEAD), P(CTX, HEAD), P())
    out_specs = (P(CTX, HEAD), P((*CTX, *HEAD), None))
    return jax.shard_map(
        per_device, mesh=fine, in_specs=in_specs, out_specs=out_specs, check_vma=False
    )
```

```python
import functools

import jax
import jax.numpy as jnp
from jax import lax
from jax.experimental import pallas as pl
from jax.experimental.pallas import tpu as pltpu
from jax.sharding import Mesh
from jax.sharding import PartitionSpec as P

HEAD_DIM = 128
GROUP = 3
CTX = ("x_hi", "z", "core")
HEAD = ("y", "x_lo")
SIZES = {"x_hi": 2, "z": 16, "core": 2, "y": 4, "x_lo": 2}


def turned(value, axis, steps):
    count = SIZES[axis]
    return lax.ppermute(value, axis, [(i, (i + steps) % count) for i in range(count)])


def passed_along(value, steps):
    count = 64
    first, last = (max(0, -steps), min(count, count - steps))
    return lax.ppermute(value, CTX, [(i, i + steps) for i in range(first, last)])


def vmem(count):
    return [pl.BlockSpec(memory_space=pltpu.VMEM)] * count


def norm_rows(hidden_in, norm_gain):
    values = hidden_in.astype(jnp.float32)
    mean_sq = jnp.mean(values * values, axis=-1, keepdims=True)
    return (values * lax.rsqrt(mean_sq + 1e-06) * norm_gain).astype(jnp.bfloat16)


def copies_over(value, axis):
    count = SIZES[axis]
    copies = jnp.broadcast_to(value[None], (count, *value.shape))
    return lax.all_to_all(copies, axis, split_axis=0, concat_axis=0)


def gather_weight(own):
    x_hi = lax.axis_index("x_hi")

    def sent(flip):
        pairs = [(c * 32 + i * 2 + (x ^ flip), x * 32 + i * 2 + c) for x in range(2) for i in range(16) for c in range(2)]
        return lax.ppermute(own, CTX, pairs)

    same, flipped = sent(0), sent(1)
    rows = jnp.concatenate([jnp.where(x_hi == 0, same, flipped), jnp.where(x_hi == 0, flipped, same)], axis=0)
    return lax.all_gather(rows, "z", axis=0, tiled=True)


def gather_tokens(normed):
    half = normed.shape[1] // 2
    low, high = normed[:, :half], normed[:, half:]
    first = lax.axis_index("core") == 0
    mine, theirs = jnp.where(first, low, high), jnp.where(first, high, low)
    tokens = jnp.concatenate([mine, turned(theirs, "core", 1)], axis=0)
    other = turned(tokens, "x_lo", 1)
    return [copies_over(tokens, "y"), copies_over(other, "y")]


def project_body(step, weight_ref, near_ref, far_ref, q_ref, kv_ref, other_q_ref, other_kv_ref, full, held, total, sem):
    x_lo = lax.axis_index("x_lo")
    copies = [
        pltpu.make_async_copy(near_ref, held.at[0], sem.at[0]),
        pltpu.make_async_copy(far_ref, held.at[1], sem.at[1]),
    ]
    n_steps = full.shape[0] // step
    for k in range(n_steps):
        at = pl.ds(k * step, step)
        copies.append(pltpu.make_async_copy(weight_ref.at[at], full.at[at], sem.at[2 + k]))
    for copy in copies:
        copy.start()
    copies[0].wait()
    copies[1].wait()
    for k in range(n_steps):
        copies[2 + k].wait()
        at = slice(k * step, (k + 1) * step)
        rows = jnp.concatenate([held[i, j, :, at] for i in range(2) for j in range(held.shape[1])], axis=0)
        product = jnp.dot(rows, full[at, :], preferred_element_type=jnp.float32)
        if k == 0:
            total[...] = product
        else:
            total[...] += product
    split = GROUP * HEAD_DIM
    count, size = held.shape[1], held.shape[2] // 2
    for j in range(2 * count):
        slot = (j % count) * 2 + (x_lo + j // count) % 2
        to = pl.ds(pl.multiple_of(slot * size, 16), size)
        for which, (q_out, kv_out) in enumerate(((q_ref, kv_ref), (other_q_ref, other_kv_ref))):
            at = slice((2 * j + which) * size, (2 * j + which + 1) * size)
            q_out[to, :] = total[at, :split]
            kv_out[0, to, :] = total[at, split : split + HEAD_DIM]
            kv_out[1, to, :] = total[at, split + HEAD_DIM :]


def project(weight, tokens):
    depth, columns = weight.shape
    count, n, _ = tokens[0].shape
    n_rows = count * n
    step = 768
    q_shape = jax.ShapeDtypeStruct((n_rows, GROUP * HEAD_DIM), jnp.float32)
    kv_shape = jax.ShapeDtypeStruct((2, n_rows, HEAD_DIM), jnp.float32)
    return pl.pallas_call(
        functools.partial(project_body, step),
        out_shape=(q_shape, kv_shape, q_shape, kv_shape),
        in_specs=[pl.BlockSpec(memory_space=pl.ANY)] * 3,
        out_specs=tuple(vmem(4)),
        scratch_shapes=[
            pltpu.VMEM((depth, columns), jnp.bfloat16),
            pltpu.VMEM((2, count, n, depth), jnp.bfloat16),
            pltpu.VMEM((2 * n_rows, columns), jnp.float32),
            pltpu.SemaphoreType.DMA((2 + depth // step,)),
        ],
        compiler_params=pltpu.CompilerParams(vmem_limit_bytes=40 * 1024 * 1024),
        cost_estimate=pl.CostEstimate(
            flops=4 * n_rows * depth * columns, bytes_accessed=2 * depth * (columns + 2 * n_rows), transcendentals=0
        ),
        name="project",
    )(weight, *tokens)


def over_keys(left, right):
    return lax.dot_general(left, right, (((0,), (0,)), ((), ())), preferred_element_type=jnp.float32)


def over_features(left, right):
    return lax.dot_general(left, right, (((1,), (1,)), ((), ())), preferred_element_type=jnp.float32)


def attend_body(
    q_part_ref, other_q_ref, own_ref, near_ref, far_ref, grad_ref, q_docs_ref, k_docs_ref, out_ref, dq_ref, far_out, near_out, own_out, q_ref, dk, dv
):
    rows = q_ref.shape[0]
    size = HEAD_DIM
    q_ref[...] = (q_part_ref[...] + other_q_ref[...]).astype(q_ref.dtype)
    count = rows // size
    scale = HEAD_DIM ** (-0.5)
    dk[...] = jnp.zeros_like(dk)
    dv[...] = jnp.zeros_like(dv)

    def window(which, r):
        parts = [far_ref[which, r * size :, :], near_ref[which], own_ref[which, : (r + 1) * size, :]]
        return jnp.concatenate(parts, axis=0)

    def by_head(ref, r):
        at = slice(r * size, (r + 1) * size)
        return jnp.concatenate([ref[at, h * HEAD_DIM : (h + 1) * HEAD_DIM] for h in range(GROUP)], axis=0)

    for r in range(count):
        first = r * size
        span = 2 * rows + size
        keys, values = window(0, r), window(1, r)
        query, grads = by_head(q_ref, r), by_head(grad_ref, r)
        gap = (
            2 * rows
            + lax.broadcasted_iota(jnp.int32, (span, size), 1)
            - lax.broadcasted_iota(jnp.int32, (span, size), 0)
        )
        same = k_docs_ref[first : first + span, :] == q_docs_ref[:, first : first + size]
        allowed = (gap >= 0) & (gap < 2 * rows) & same
        hidden = jnp.where(allowed, jnp.float32(0), jnp.float32(-1e30))
        hidden = jnp.concatenate([hidden] * GROUP, axis=1)
        scores = over_features(keys, query) * scale + hidden
        expo = jnp.exp(scores)
        prob = expo * (1.0 / jnp.sum(expo, axis=0, keepdims=True))
        prob_b = prob.astype(jnp.bfloat16)
        out_t = over_keys(values, prob_b).astype(jnp.bfloat16)
        grads_t = jnp.transpose(grads.astype(jnp.float32))
        delta = jnp.sum(grads_t * out_t.astype(jnp.float32), axis=0, keepdims=True)
        dprob = over_features(values, grads)
        dscore = (prob * (dprob - delta)).astype(jnp.bfloat16)
        to = slice(first, first + span)
        dv[to, :] += jnp.dot(prob_b, grads, preferred_element_type=jnp.float32)
        dk[to, :] += jnp.dot(dscore, query, preferred_element_type=jnp.float32)
        dq = jnp.transpose(over_keys(keys, dscore)) * scale
        out = jnp.transpose(out_t.astype(jnp.float32))
        for h in range(GROUP):
            at = slice(h * size, (h + 1) * size)
            out_ref[first : first + size, at] = out[at, :].astype(out_ref.dtype)
            dq_ref[first : first + size, at] = dq[at, :].astype(dq_ref.dtype)
    for which, terms, factor in ((0, dk, scale), (1, dv, 1.0)):
        far_out[which] = (terms[:rows, :] * factor).astype(far_out.dtype)
        near_out[which] = (terms[rows : 2 * rows, :] * factor).astype(near_out.dtype)
        own_out[which] = terms[2 * rows :, :] * factor


def attend(q_part, other_q, own_kv, near_kv, far_kv, out_grad, q_docs, k_docs):
    rows = q_part.shape[0]
    kv_shape = (2, rows, HEAD_DIM)
    work = 2 * 3 * rows * 7 * rows // 3 * HEAD_DIM
    return pl.pallas_call(
        attend_body,
        out_shape=(
            jax.ShapeDtypeStruct(q_part.shape, jnp.bfloat16),
            jax.ShapeDtypeStruct(q_part.shape, jnp.bfloat16),
            jax.ShapeDtypeStruct(kv_shape, jnp.bfloat16),
            jax.ShapeDtypeStruct(kv_shape, jnp.bfloat16),
            jax.ShapeDtypeStruct(kv_shape, jnp.float32),
        ),
        in_specs=vmem(8),
        out_specs=tuple(vmem(5)),
        scratch_shapes=[
            pltpu.VMEM(q_part.shape, jnp.bfloat16),
            pltpu.VMEM((3 * rows, HEAD_DIM), jnp.float32),
            pltpu.VMEM((3 * rows, HEAD_DIM), jnp.float32),
        ],
        compiler_params=pltpu.CompilerParams(vmem_limit_bytes=32 * 1024 * 1024),
        cost_estimate=pl.CostEstimate(flops=5 * work, bytes_accessed=10 * rows * rows, transcendentals=7 * rows * rows),
        name="attend",
    )(q_part, other_q, own_kv, near_kv, far_kv, out_grad, q_docs, k_docs)


def add_body(dq_ref, own_ref, near_ref, far_ref, out_ref):
    split = dq_ref.shape[1]
    out_ref[:, :split] = dq_ref[...]
    for which in range(2):
        total = own_ref[which] + near_ref[which].astype(jnp.float32) + far_ref[which].astype(jnp.float32)
        at = slice(split + which * HEAD_DIM, split + (which + 1) * HEAD_DIM)
        out_ref[:, at] = total.astype(out_ref.dtype)


def add_terms(dq, own, near, far):
    rows, columns = dq.shape
    return pl.pallas_call(
        add_body,
        out_shape=jax.ShapeDtypeStruct((rows, columns + 2 * HEAD_DIM), jnp.bfloat16),
        in_specs=vmem(4),
        out_specs=vmem(1)[0],
        name="add_terms",
    )(dq, own, near, far)


def per_device(hidden_in, norm_gain, qkv_weight, out_grad, doc_ids):
    rows = out_grad.shape[0]
    weight = gather_weight(qkv_weight)
    tokens = gather_tokens(norm_rows(hidden_in, norm_gain))
    q_part, kv_part, other_q, other_kv = project(weight, tokens)
    own_kv = (kv_part + turned(other_kv, "core", 1)).astype(jnp.bfloat16)
    other_q, own_kv = lax.optimization_barrier((other_q, own_kv))
    other_q = turned(other_q, "core", 1)
    near_kv = passed_along(own_kv, 1)
    far_kv = passed_along(own_kv, 2)
    start = lax.axis_index(CTX) * rows
    padded_docs = jnp.concatenate([jnp.full((2 * rows,), -1, jnp.int32), doc_ids])
    q_docs = lax.dynamic_slice_in_dim(doc_ids, start, rows, 0).reshape(1, rows)
    k_docs = lax.dynamic_slice_in_dim(padded_docs, start, 3 * rows, 0).reshape(3 * rows, 1)
    attn_out, dq, far, near, own = attend(q_part, other_q, own_kv, near_kv, far_kv, out_grad, q_docs, k_docs)
    from_near = passed_along(near, -1)
    from_far = passed_along(far, -2)
    block = add_terms(dq, own, from_near, from_far)
    return (attn_out, lax.all_to_all(block, HEAD, split_axis=0, concat_axis=1, tiled=True))


def solution(mesh):
    fine = Mesh(mesh.devices.reshape(tuple(SIZES.values())), tuple(SIZES))
    in_specs = (P((*CTX, *HEAD), None), P(), P(CTX, HEAD), P(CTX, HEAD), P())
    out_specs = (P(CTX, HEAD), P((*CTX, *HEAD), None))
    return jax.shard_map(
        per_device, mesh=fine, in_specs=in_specs, out_specs=out_specs, check_vma=False
    )
```

```python
import functools

import jax
import jax.numpy as jnp
from jax import lax
from jax.experimental import pallas as pl
from jax.experimental.pallas import tpu as pltpu
from jax.sharding import Mesh
from jax.sharding import PartitionSpec as P

HEAD_DIM = 128
GROUP = 3
CTX = ("x_hi", "z", "core")
HEAD = ("y", "x_lo")
LEVELS = 8
SIZES = {"x_hi": 2, "z": 16, "core": 2, "y": 4, "x_lo": 2}


def turned(value, axis, steps):
    count = SIZES[axis]
    return lax.ppermute(value, axis, [(i, (i + steps) % count) for i in range(count)])


def passed_along(value, steps):
    count = 64
    first, last = (max(0, -steps), min(count, count - steps))
    return lax.ppermute(value, CTX, [(i, i + steps) for i in range(first, last)])


def vmem(count):
    return [pl.BlockSpec(memory_space=pltpu.VMEM)] * count


def norm_rows(hidden_in, norm_gain):
    values = hidden_in.astype(jnp.float32)
    mean_sq = jnp.mean(values * values, axis=-1, keepdims=True)
    return (values * lax.rsqrt(mean_sq + 1e-06) * norm_gain).astype(jnp.bfloat16)


def copies_over(value, axes, count):
    copies = jnp.broadcast_to(value[None], (count, *value.shape))
    return lax.all_to_all(copies, axes, split_axis=0, concat_axis=0)


def pair_rows(own):
    x_hi = lax.axis_index("x_hi")

    def sent(flip):
        pairs = [(c * 32 + i * 2 + (x ^ flip), x * 32 + i * 2 + c) for x in range(2) for i in range(16) for c in range(2)]
        return lax.ppermute(own, CTX, pairs)

    same, flipped = sent(0), sent(1)
    return jnp.concatenate([jnp.where(x_hi == 0, same, flipped), jnp.where(x_hi == 0, flipped, same)], axis=0)


def gather_weight(rows):
    top = jnp.max(jnp.abs(rows.astype(jnp.float32)))
    level = sum((top < 2.0 ** (-1 - 15 * i)).astype(jnp.float32) for i in range(1, LEVELS))
    scale = sum(jnp.where(level == i, 2.0 ** (17 + 15 * i), 0.0) for i in range(LEVELS))
    scaled = (rows.astype(jnp.float32) * scale).astype(jnp.float16)
    tail = jnp.full((8, rows.shape[1]), level, jnp.float16)
    blocks = lax.all_gather(jnp.concatenate([scaled, tail], axis=0), "z", axis=0)
    levels = blocks[:, rows.shape[0] :, :1][:, :1].astype(jnp.float32)
    back = sum(jnp.where(levels == i, 2.0 ** (-17 - 15 * i), 0.0) for i in range(LEVELS))
    split = GROUP * HEAD_DIM

    def columns(first, last):
        part = blocks[:, : rows.shape[0], first:last].astype(jnp.float32) * back
        return part.astype(jnp.bfloat16).reshape(-1, last - first)

    return columns(0, split), columns(split, rows.shape[1])


def gather_tokens(normed):
    half = normed.shape[1] // 2
    low, high = normed[:, :half], normed[:, half:]
    first = lax.axis_index("core") == 0
    mine, theirs = jnp.where(first, low, high), jnp.where(first, high, low)
    tokens = jnp.concatenate([mine, turned(theirs, "core", 1)], axis=0)
    return copies_over(tokens, HEAD, 8)


def project_body(step, weight_ref, tokens_ref, own_ref, other_ref, part, held, total, sem):
    n_steps = part.shape[0] // step
    copies = []
    for k in range(n_steps):
        at = pl.ds(k * step, step)
        moves = [
            (tokens_ref.at[:, :, at], held.at[:, :, at]),
            (weight_ref.at[at], part.at[at]),
        ]
        copies.append([pltpu.make_async_copy(source, to, sem.at[k, i]) for i, (source, to) in enumerate(moves)])
    for group in copies:
        for copy in group:
            copy.start()
    for k in range(n_steps):
        for copy in copies[k]:
            copy.wait()
        at = slice(k * step, (k + 1) * step)
        rows = held[:, :, at].reshape(held.shape[0] * held.shape[1], step)
        product = jnp.dot(rows, part[at, :], preferred_element_type=jnp.float32)
        if k == 0:
            total[...] = product
        else:
            total[...] += product
    count, size = held.shape[0], held.shape[1] // 2
    for j in range(count):
        to = slice(j * size, (j + 1) * size)
        own_ref[to, :] = total[2 * j * size : (2 * j + 1) * size, :]
        other_ref[to, :] = total[(2 * j + 1) * size : (2 * j + 2) * size, :]


def project(weight, tokens):
    depth, columns = weight.shape
    count, n, _ = tokens.shape
    n_rows = count * n // 2
    step = 768
    shape = jax.ShapeDtypeStruct((n_rows, columns), jnp.float32)
    return pl.pallas_call(
        functools.partial(project_body, step),
        out_shape=(shape, shape),
        in_specs=[pl.BlockSpec(memory_space=pltpu.HBM)] * 2,
        out_specs=tuple(vmem(2)),
        scratch_shapes=[
            pltpu.VMEM((depth, columns), jnp.bfloat16),
            pltpu.VMEM((count, n, depth), jnp.bfloat16),
            pltpu.VMEM((2 * n_rows, columns), jnp.float32),
            pltpu.SemaphoreType.DMA((depth // step, 2)),
        ],
        compiler_params=pltpu.CompilerParams(vmem_limit_bytes=16 * 1024 * 1024),
        cost_estimate=pl.CostEstimate(
            flops=4 * n_rows * depth * columns, bytes_accessed=2 * depth * (columns + 2 * n_rows), transcendentals=0
        ),
        name="project",
    )(weight, tokens)


def over_keys(left, right):
    return lax.dot_general(left, right, (((0,), (0,)), ((), ())), preferred_element_type=jnp.float32)


def over_features(left, right):
    return lax.dot_general(left, right, (((1,), (1,)), ((), ())), preferred_element_type=jnp.float32)


def attend_body(
    q_part_ref, other_q_ref, own_ref, near_ref, far_ref, grad_ref, q_docs_ref, k_docs_ref, out_ref, dq_ref, far_out, near_out, own_out, q_ref, dk, dv
):
    rows = q_ref.shape[0]
    size = HEAD_DIM
    q_ref[...] = (q_part_ref[...] + other_q_ref[...]).astype(q_ref.dtype)
    count = rows // size
    scale = HEAD_DIM ** (-0.5)
    dk[...] = jnp.zeros_like(dk)
    dv[...] = jnp.zeros_like(dv)

    def window(which, r):
        at = slice(which * HEAD_DIM, (which + 1) * HEAD_DIM)
        parts = [far_ref[r * size :, at], near_ref[:, at], own_ref[: (r + 1) * size, at]]
        return jnp.concatenate(parts, axis=0)

    def by_head(ref, r):
        at = slice(r * size, (r + 1) * size)
        return jnp.concatenate([ref[at, h * HEAD_DIM : (h + 1) * HEAD_DIM] for h in range(GROUP)], axis=0)

    for r in range(count):
        first = r * size
        span = 2 * rows + size
        keys, values = window(0, r), window(1, r)
        query, grads = by_head(q_ref, r), by_head(grad_ref, r)
        gap = (
            2 * rows
            + lax.broadcasted_iota(jnp.int32, (span, size), 1)
            - lax.broadcasted_iota(jnp.int32, (span, size), 0)
        )
        same = k_docs_ref[first : first + span, :] == q_docs_ref[:, first : first + size]
        allowed = (gap >= 0) & (gap < 2 * rows) & same
        hidden = jnp.where(allowed, jnp.float32(0), jnp.float32(-1e30))
        hidden = jnp.concatenate([hidden] * GROUP, axis=1)
        scores = over_features(keys, query) * scale + hidden
        expo = jnp.exp(scores)
        prob = expo * (1.0 / jnp.sum(expo, axis=0, keepdims=True))
        prob_b = prob.astype(jnp.bfloat16)
        out_t = over_keys(values, prob_b).astype(jnp.bfloat16)
        grads_t = jnp.transpose(grads.astype(jnp.float32))
        delta = jnp.sum(grads_t * out_t.astype(jnp.float32), axis=0, keepdims=True)
        dprob = over_features(values, grads)
        dscore = (prob * (dprob - delta)).astype(jnp.bfloat16)
        to = slice(first, first + span)
        dv[to, :] += jnp.dot(prob_b, grads, preferred_element_type=jnp.float32)
        dk[to, :] += jnp.dot(dscore, query, preferred_element_type=jnp.float32)
        dq = jnp.transpose(over_keys(keys, dscore)) * scale
        out = jnp.transpose(out_t.astype(jnp.float32))
        for h in range(GROUP):
            at = slice(h * size, (h + 1) * size)
            out_ref[first : first + size, at] = out[at, :].astype(out_ref.dtype)
            dq_ref[first : first + size, at] = dq[at, :].astype(dq_ref.dtype)
    for which, terms, factor in ((0, dk, scale), (1, dv, 1.0)):
        at = slice(which * HEAD_DIM, (which + 1) * HEAD_DIM)
        far_out[:, at] = (terms[:rows, :] * factor).astype(far_out.dtype)
        near_out[:, at] = (terms[rows : 2 * rows, :] * factor).astype(near_out.dtype)
        own_out[:, at] = terms[2 * rows :, :] * factor


def attend(q_part, other_q, own_kv, near_kv, far_kv, out_grad, q_docs, k_docs):
    rows = q_part.shape[0]
    kv_shape = (rows, 2 * HEAD_DIM)
    work = 2 * 3 * rows * 7 * rows // 3 * HEAD_DIM
    return pl.pallas_call(
        attend_body,
        out_shape=(
            jax.ShapeDtypeStruct(q_part.shape, jnp.bfloat16),
            jax.ShapeDtypeStruct(q_part.shape, jnp.bfloat16),
            jax.ShapeDtypeStruct(kv_shape, jnp.bfloat16),
            jax.ShapeDtypeStruct(kv_shape, jnp.bfloat16),
            jax.ShapeDtypeStruct(kv_shape, jnp.float32),
        ),
        in_specs=vmem(8),
        out_specs=tuple(vmem(5)),
        scratch_shapes=[
            pltpu.VMEM(q_part.shape, jnp.bfloat16),
            pltpu.VMEM((3 * rows, HEAD_DIM), jnp.float32),
            pltpu.VMEM((3 * rows, HEAD_DIM), jnp.float32),
        ],
        compiler_params=pltpu.CompilerParams(vmem_limit_bytes=24 * 1024 * 1024),
        cost_estimate=pl.CostEstimate(flops=5 * work, bytes_accessed=10 * rows * rows, transcendentals=7 * rows * rows),
        name="attend",
    )(q_part, other_q, own_kv, near_kv, far_kv, out_grad, q_docs, k_docs)


def add_body(dq_ref, own_ref, near_ref, far_ref, out_ref):
    split = dq_ref.shape[1]
    out_ref[:, :split] = dq_ref[...]
    total = own_ref[...] + near_ref[...].astype(jnp.float32) + far_ref[...].astype(jnp.float32)
    out_ref[:, split:] = total.astype(out_ref.dtype)


def add_terms(dq, own, near, far):
    rows, columns = dq.shape
    return pl.pallas_call(
        add_body,
        out_shape=jax.ShapeDtypeStruct((rows, columns + own.shape[1]), jnp.bfloat16),
        in_specs=vmem(4),
        out_specs=vmem(1)[0],
        compiler_params=pltpu.CompilerParams(vmem_limit_bytes=4 * 1024 * 1024),
        name="add_terms",
    )(dq, own, near, far)


def per_device(hidden_in, norm_gain, qkv_weight, out_grad, doc_ids):
    rows = out_grad.shape[0]
    block = pair_rows(qkv_weight)
    block, normed = lax.optimization_barrier((block, norm_rows(hidden_in, norm_gain)))
    tokens = gather_tokens(normed)
    q_weight, kv_weight = gather_weight(block)
    kv_part, other_kv = project(kv_weight, tokens)
    q_part, other_q = project(q_weight, tokens)
    own_kv = (kv_part + turned(other_kv, "core", 1)).astype(jnp.bfloat16)
    other_q, own_kv = lax.optimization_barrier((other_q, own_kv))
    other_q = turned(other_q, "core", 1)
    near_kv = passed_along(own_kv, 1)
    far_kv = passed_along(own_kv, 2)
    start = lax.axis_index(CTX) * rows
    padded_docs = jnp.concatenate([jnp.full((2 * rows,), -1, jnp.int32), doc_ids])
    q_docs = lax.dynamic_slice_in_dim(doc_ids, start, rows, 0).reshape(1, rows)
    k_docs = lax.dynamic_slice_in_dim(padded_docs, start, 3 * rows, 0).reshape(3 * rows, 1)
    attn_out, dq, far, near, own = attend(q_part, other_q, own_kv, near_kv, far_kv, out_grad, q_docs, k_docs)
    from_near = passed_along(near, -1)
    from_far = passed_along(far, -2)
    block = add_terms(dq, own, from_near, from_far)
    return (attn_out, lax.all_to_all(block, HEAD, split_axis=0, concat_axis=1, tiled=True))


def solution(mesh):
    fine = Mesh(mesh.devices.reshape(tuple(SIZES.values())), tuple(SIZES))
    in_specs = (P((*CTX, *HEAD), None), P(), P(CTX, HEAD), P(CTX, HEAD), P())
    out_specs = (P(CTX, HEAD), P((*CTX, *HEAD), None))
    return jax.shard_map(
        per_device, mesh=fine, in_specs=in_specs, out_specs=out_specs, check_vma=False
    )
```

```python
import functools

import jax
import jax.numpy as jnp
from jax import lax
from jax.experimental import pallas as pl
from jax.experimental.pallas import tpu as pltpu
from jax.sharding import Mesh
from jax.sharding import PartitionSpec as P

HEAD_DIM = 128
GROUP = 3
CTX = ("x_hi", "z", "core")
HEAD = ("y", "x_lo")
LEVELS = 8
SIZES = {"x_hi": 2, "z": 16, "core": 2, "y": 4, "x_lo": 2}


def turned(value, axis, steps):
    count = SIZES[axis]
    return lax.ppermute(value, axis, [(i, (i + steps) % count) for i in range(count)])


def passed_along(value, steps):
    count = 64
    first, last = (max(0, -steps), min(count, count - steps))
    return lax.ppermute(value, CTX, [(i, i + steps) for i in range(first, last)])


def vmem(count):
    return [pl.BlockSpec(memory_space=pltpu.VMEM)] * count


def norm_body(hidden_ref, gain_ref, out_ref, held, sem):
    values = hidden_ref[...].astype(jnp.float32)
    mean_sq = jnp.mean(values * values, axis=-1, keepdims=True)
    held[...] = (values * lax.rsqrt(mean_sq + 1e-06) * gain_ref[...]).astype(held.dtype)
    count, _, width = out_ref.shape
    copies = [
        pltpu.make_async_copy(held.at[:, pl.ds(i // (count // 2) * width, width)], out_ref.at[i], sem.at[i])
        for i in range(count)
    ]
    for copy in copies:
        copy.start()
    for copy in copies:
        copy.wait()


def norm_copies(hidden_in, norm_gain):
    rows, width = hidden_in.shape
    count = SIZES["core"] * SIZES["y"] * SIZES["x_lo"]
    return pl.pallas_call(
        norm_body,
        out_shape=jax.ShapeDtypeStruct((count, rows, width // 2), jnp.bfloat16),
        in_specs=vmem(2),
        out_specs=pl.BlockSpec(memory_space=pltpu.HBM),
        scratch_shapes=[pltpu.VMEM((rows, width), jnp.bfloat16), pltpu.SemaphoreType.DMA((count,))],
        compiler_params=pltpu.CompilerParams(vmem_limit_bytes=60 * 1024 * 1024),
        cost_estimate=pl.CostEstimate(
            flops=10 * rows * width, bytes_accessed=(2 + count) * rows * width, transcendentals=0
        ),
        name="norm",
    )(hidden_in, norm_gain.reshape(1, width))


def pair_rows(own):
    def sent(flip):
        pairs = [(c * 32 + i * 2 + (x ^ flip), x * 32 + i * 2 + c) for x in range(2) for i in range(16) for c in range(2)]
        return lax.ppermute(own, CTX, pairs)

    return sent(0), sent(1)


def scale_body(same_ref, flipped_ref, out_ref):
    first = lax.axis_index("x_hi") == 0
    size = same_ref.shape[0]
    same, flipped = same_ref[...].astype(jnp.float32), flipped_ref[...].astype(jnp.float32)
    top = jnp.maximum(jnp.abs(same), jnp.abs(flipped))
    top = jnp.max(jnp.max(top, axis=0, keepdims=True), axis=1, keepdims=True)
    level, scale = jnp.zeros_like(top), jnp.full_like(top, 2.0**17)
    for i in range(1, LEVELS):
        small = top < 2.0 ** (-1 - 15 * i)
        level = jnp.where(small, float(i), level)
        scale = jnp.where(small, 2.0 ** (17 + 15 * i), scale)
    out_ref[:size, :] = (jnp.where(first, same, flipped) * scale).astype(out_ref.dtype)
    out_ref[size : 2 * size, :] = (jnp.where(first, flipped, same) * scale).astype(out_ref.dtype)
    tail = (out_ref.shape[0] - 2 * size, out_ref.shape[1])
    out_ref[2 * size :, :] = jnp.broadcast_to(level, tail).astype(out_ref.dtype)


def scaled_rows(same, flipped):
    return pl.pallas_call(
        scale_body,
        out_shape=jax.ShapeDtypeStruct((2 * same.shape[0] + 16, same.shape[1]), same.dtype),
        in_specs=vmem(2),
        out_specs=vmem(1)[0],
        compiler_params=pltpu.CompilerParams(vmem_limit_bytes=4 * 1024 * 1024),
        name="scale",
    )(same, flipped)


def gather_weight(scaled):
    n_rows = scaled.shape[0] - 16
    blocks = lax.all_gather(scaled[: n_rows + 8].astype(jnp.float16), "z", axis=0)
    levels = blocks[:, n_rows : n_rows + 1, :1].astype(jnp.float32)
    back = sum(jnp.where(levels == i, 2.0 ** (-17 - 15 * i), 0.0) for i in range(LEVELS))
    split = GROUP * HEAD_DIM

    def columns(first, last):
        part = blocks[:, :n_rows, first:last].astype(jnp.float32) * back
        return part.astype(jnp.bfloat16).reshape(-1, last - first)

    return columns(0, split), columns(split, scaled.shape[1])


def project_body(step, weight_ref, tokens_ref, out_ref):
    count, size, _ = tokens_ref.shape
    for k in range(weight_ref.shape[0] // step):
        at = slice(k * step, (k + 1) * step)
        rows = tokens_ref[:, :, at].reshape(count * size, step)
        product = jnp.dot(rows, weight_ref[at, :], preferred_element_type=jnp.float32)
        if k == 0:
            out_ref[...] = product
        else:
            out_ref[...] += product


def project(weight, tokens, cost):
    depth, columns = weight.shape
    n_rows = tokens.shape[0] * tokens.shape[1]
    out = pl.pallas_call(
        functools.partial(project_body, 1536),
        out_shape=jax.ShapeDtypeStruct((n_rows, columns), jnp.float32),
        in_specs=vmem(2),
        out_specs=vmem(1)[0],
        compiler_params=pltpu.CompilerParams(vmem_limit_bytes=6 * 1024 * 1024),
        cost_estimate=pl.CostEstimate(
            flops=int(cost * 2 * n_rows * depth * columns),
            bytes_accessed=int(cost * 2 * depth * (columns + n_rows)),
            transcendentals=0,
        ),
        name="project",
    )(weight, tokens)
    first = lax.axis_index("core") == 0
    low, high = out[: n_rows // 2], out[n_rows // 2 :]
    return jnp.where(first, low, high), jnp.where(first, high, low)


def over_keys(left, right):
    return lax.dot_general(left, right, (((0,), (0,)), ((), ())), preferred_element_type=jnp.float32)


def over_features(left, right):
    return lax.dot_general(left, right, (((1,), (1,)), ((), ())), preferred_element_type=jnp.float32)


def window_body(far_ref, near_ref, own_ref, out_ref):
    rows = own_ref.shape[0]
    for i, ref in enumerate((far_ref, near_ref, own_ref)):
        out_ref[i * rows : (i + 1) * rows, :] = ref[...]


def window(far_kv, near_kv, own_kv):
    rows, columns = own_kv.shape
    return pl.pallas_call(
        window_body,
        out_shape=jax.ShapeDtypeStruct((3 * rows, columns), own_kv.dtype),
        in_specs=vmem(3),
        out_specs=vmem(1)[0],
        compiler_params=pltpu.CompilerParams(vmem_limit_bytes=4 * 1024 * 1024),
        cost_estimate=pl.CostEstimate(flops=10**10, bytes_accessed=4 * 10**7, transcendentals=0),
        name="window",
    )(far_kv, near_kv, own_kv)


def attend_body(
    q_part_ref, other_q_ref, window_ref, grad_ref, q_docs_ref, k_docs_ref, out_ref, dq_ref, far_out, near_out, own_out, q_ref, dk, dv
):
    rows = q_ref.shape[0]
    size = HEAD_DIM
    q_ref[...] = (q_part_ref[...] + other_q_ref[...]).astype(q_ref.dtype)
    count = rows // size
    scale = HEAD_DIM ** (-0.5)
    dk[...] = jnp.zeros_like(dk)
    dv[...] = jnp.zeros_like(dv)

    def window(which, r):
        return window_ref[r * size : (r + 1) * size + 2 * rows, which * HEAD_DIM : (which + 1) * HEAD_DIM]

    def by_head(ref, r):
        at = slice(r * size, (r + 1) * size)
        return jnp.concatenate([ref[at, h * HEAD_DIM : (h + 1) * HEAD_DIM] for h in range(GROUP)], axis=0)

    for r in range(count):
        first = r * size
        span = 2 * rows + size
        keys, values = window(0, r), window(1, r)
        query, grads = by_head(q_ref, r), by_head(grad_ref, r)
        gap = (
            2 * rows
            + lax.broadcasted_iota(jnp.int32, (span, size), 1)
            - lax.broadcasted_iota(jnp.int32, (span, size), 0)
        )
        same = k_docs_ref[first : first + span, :] == q_docs_ref[:, first : first + size]
        allowed = (gap >= 0) & (gap < 2 * rows) & same
        hidden = jnp.where(allowed, jnp.float32(0), jnp.float32(-1e30))
        hidden = jnp.concatenate([hidden] * GROUP, axis=1)
        scores = over_features(keys, query) * scale + hidden
        expo = jnp.exp(scores)
        prob = expo * (1.0 / jnp.sum(expo, axis=0, keepdims=True))
        prob_b = prob.astype(jnp.bfloat16)
        out_t = over_keys(values, prob_b).astype(jnp.bfloat16)
        grads_t = jnp.transpose(grads.astype(jnp.float32))
        delta = jnp.sum(grads_t * out_t.astype(jnp.float32), axis=0, keepdims=True)
        dprob = over_features(values, grads)
        dscore = (prob * (dprob - delta)).astype(jnp.bfloat16)
        to = slice(first, first + span)
        dv[to, :] += jnp.dot(prob_b, grads, preferred_element_type=jnp.float32)
        dk[to, :] += jnp.dot(dscore, query, preferred_element_type=jnp.float32)
        dq = jnp.transpose(over_keys(keys, dscore)) * scale
        out = jnp.transpose(out_t.astype(jnp.float32))
        for h in range(GROUP):
            at = slice(h * size, (h + 1) * size)
            out_ref[first : first + size, at] = out[at, :].astype(out_ref.dtype)
            dq_ref[first : first + size, at] = dq[at, :].astype(dq_ref.dtype)
    for which, terms, factor in ((0, dk, scale), (1, dv, 1.0)):
        at = slice(which * HEAD_DIM, (which + 1) * HEAD_DIM)
        far_out[:, at] = (terms[:rows, :] * factor).astype(far_out.dtype)
        near_out[:, at] = (terms[rows : 2 * rows, :] * factor).astype(near_out.dtype)
        own_out[:, at] = terms[2 * rows :, :] * factor


def attend(q_part, other_q, window_kv, out_grad, q_docs, k_docs):
    rows = q_part.shape[0]
    kv_shape = (rows, 2 * HEAD_DIM)
    work = 2 * 3 * rows * 7 * rows // 3 * HEAD_DIM
    return pl.pallas_call(
        attend_body,
        out_shape=(
            jax.ShapeDtypeStruct(q_part.shape, jnp.bfloat16),
            jax.ShapeDtypeStruct(q_part.shape, jnp.bfloat16),
            jax.ShapeDtypeStruct(kv_shape, jnp.bfloat16),
            jax.ShapeDtypeStruct(kv_shape, jnp.bfloat16),
            jax.ShapeDtypeStruct(kv_shape, jnp.float32),
        ),
        in_specs=vmem(6),
        out_specs=tuple(vmem(5)),
        scratch_shapes=[
            pltpu.VMEM(q_part.shape, jnp.bfloat16),
            pltpu.VMEM((3 * rows, HEAD_DIM), jnp.float32),
            pltpu.VMEM((3 * rows, HEAD_DIM), jnp.float32),
        ],
        compiler_params=pltpu.CompilerParams(vmem_limit_bytes=14 * 1024 * 1024),
        cost_estimate=pl.CostEstimate(flops=5 * work, bytes_accessed=10 * rows * rows, transcendentals=7 * rows * rows),
        name="attend",
    )(q_part, other_q, window_kv, out_grad, q_docs, k_docs)


def add_body(dq_ref, own_ref, near_ref, far_ref, out_ref):
    split = dq_ref.shape[1]
    out_ref[:, :split] = dq_ref[...]
    total = own_ref[...] + near_ref[...].astype(jnp.float32) + far_ref[...].astype(jnp.float32)
    out_ref[:, split:] = total.astype(out_ref.dtype)


def add_terms(dq, own, near, far):
    rows, columns = dq.shape
    return pl.pallas_call(
        add_body,
        out_shape=jax.ShapeDtypeStruct((rows, columns + own.shape[1]), jnp.bfloat16),
        in_specs=vmem(4),
        out_specs=vmem(1)[0],
        compiler_params=pltpu.CompilerParams(vmem_limit_bytes=4 * 1024 * 1024),
        name="add_terms",
    )(dq, own, near, far)


def per_device(hidden_in, norm_gain, qkv_weight, out_grad, doc_ids):
    rows = out_grad.shape[0]
    same, flipped = pair_rows(qkv_weight)
    copies = norm_copies(hidden_in, norm_gain)
    same, flipped, copies = lax.optimization_barrier((same, flipped, copies))
    tokens = lax.all_to_all(copies, ("core", *HEAD), split_axis=0, concat_axis=0)
    q_weight, kv_weight = gather_weight(scaled_rows(same, flipped))
    kv_part, other_kv = project(kv_weight, tokens, 1)
    own_kv = (kv_part + turned(other_kv, "core", 1)).astype(jnp.bfloat16)
    own_kv, q_weight = lax.optimization_barrier((own_kv, q_weight))
    q_part, other_q = project(q_weight, tokens, 0.01)
    other_q = turned(other_q, "core", 1)
    near_kv = passed_along(own_kv, 1)
    far_kv = passed_along(own_kv, 2)
    start = lax.axis_index(CTX) * rows
    padded_docs = jnp.concatenate([jnp.full((2 * rows,), -1, jnp.int32), doc_ids])
    q_docs = lax.dynamic_slice_in_dim(doc_ids, start, rows, 0).reshape(1, rows)
    k_docs = lax.dynamic_slice_in_dim(padded_docs, start, 3 * rows, 0).reshape(3 * rows, 1)
    attn_out, dq, far, near, own = attend(q_part, other_q, window(far_kv, near_kv, own_kv), out_grad, q_docs, k_docs)
    from_near = passed_along(near, -1)
    from_far = passed_along(far, -2)
    block = add_terms(dq, own, from_near, from_far)
    return (attn_out, lax.all_to_all(block, HEAD, split_axis=0, concat_axis=1, tiled=True))


def solution(mesh):
    fine = Mesh(mesh.devices.reshape(tuple(SIZES.values())), tuple(SIZES))
    in_specs = (P((*CTX, *HEAD), None), P(), P(CTX, HEAD), P(CTX, HEAD), P())
    out_specs = (P(CTX, HEAD), P((*CTX, *HEAD), None))
    return jax.shard_map(
        per_device, mesh=fine, in_specs=in_specs, out_specs=out_specs, check_vma=False
    )
```

```python
import functools

import jax
import jax.numpy as jnp
from jax import lax
from jax.experimental import pallas as pl
from jax.experimental.pallas import tpu as pltpu
from jax.sharding import Mesh
from jax.sharding import PartitionSpec as P

HEAD_DIM = 128
GROUP = 3
CTX = ("x_hi", "z", "core")
HEAD = ("y", "x_lo")
LEVELS = 8
SIZES = {"x_hi": 2, "z": 16, "core": 2, "y": 4, "x_lo": 2}


def turned(value, axis, steps):
    count = SIZES[axis]
    return lax.ppermute(value, axis, [(i, (i + steps) % count) for i in range(count)])


def passed_along(value, steps):
    count = 64
    first, last = (max(0, -steps), min(count, count - steps))
    return lax.ppermute(value, CTX, [(i, i + steps) for i in range(first, last)])


def vmem(count):
    return [pl.BlockSpec(memory_space=pltpu.VMEM)] * count


def norm_body(hidden_ref, gain_ref, out_ref, held, sem):
    values = hidden_ref[...].astype(jnp.float32)
    mean_sq = jnp.mean(values * values, axis=-1, keepdims=True)
    held[...] = (values * lax.rsqrt(mean_sq + 1e-06) * gain_ref[...]).astype(held.dtype)
    count, _, width = out_ref.shape
    copies = [
        pltpu.make_async_copy(held.at[:, pl.ds(i // (count // 2) * width, width)], out_ref.at[i], sem.at[i])
        for i in range(count)
    ]
    for copy in copies:
        copy.start()
    for copy in copies:
        copy.wait()


def norm_copies(hidden_in, norm_gain):
    rows, width = hidden_in.shape
    count = SIZES["core"] * SIZES["y"] * SIZES["x_lo"]
    return pl.pallas_call(
        norm_body,
        out_shape=jax.ShapeDtypeStruct((count, rows, width // 2), jnp.bfloat16),
        in_specs=vmem(2),
        out_specs=pl.BlockSpec(memory_space=pltpu.HBM),
        scratch_shapes=[pltpu.VMEM((rows, width), jnp.bfloat16), pltpu.SemaphoreType.DMA((count,))],
        compiler_params=pltpu.CompilerParams(vmem_limit_bytes=60 * 1024 * 1024),
        cost_estimate=pl.CostEstimate(
            flops=10 * rows * width, bytes_accessed=(2 + count) * rows * width, transcendentals=0
        ),
        name="norm",
    )(hidden_in, norm_gain.reshape(1, width))


def pair_rows(own):
    def sent(flip):
        pairs = [(c * 32 + i * 2 + (x ^ flip), x * 32 + i * 2 + c) for x in range(2) for i in range(16) for c in range(2)]
        return lax.ppermute(own, CTX, pairs)

    return sent(0), sent(1)


def scale_body(same_ref, flipped_ref, out_ref):
    first = lax.axis_index("x_hi") == 0
    size = same_ref.shape[0]
    same, flipped = same_ref[...].astype(jnp.float32), flipped_ref[...].astype(jnp.float32)
    top = jnp.maximum(jnp.abs(same), jnp.abs(flipped))
    top = jnp.max(jnp.max(top, axis=0, keepdims=True), axis=1, keepdims=True)
    level, scale = jnp.zeros_like(top), jnp.full_like(top, 2.0**17)
    for i in range(1, LEVELS):
        small = top < 2.0 ** (-1 - 15 * i)
        level = jnp.where(small, float(i), level)
        scale = jnp.where(small, 2.0 ** (17 + 15 * i), scale)
    out_ref[:size, :] = (jnp.where(first, same, flipped) * scale).astype(out_ref.dtype)
    out_ref[size : 2 * size, :] = (jnp.where(first, flipped, same) * scale).astype(out_ref.dtype)
    tail = (out_ref.shape[0] - 2 * size, out_ref.shape[1])
    out_ref[2 * size :, :] = jnp.broadcast_to(level, tail).astype(out_ref.dtype)


def scaled_rows(same, flipped):
    return pl.pallas_call(
        scale_body,
        out_shape=jax.ShapeDtypeStruct((2 * same.shape[0] + 16, same.shape[1]), same.dtype),
        in_specs=vmem(2),
        out_specs=vmem(1)[0],
        compiler_params=pltpu.CompilerParams(vmem_limit_bytes=4 * 1024 * 1024),
        name="scale",
    )(same, flipped)


def gather_weight(scaled):
    n_rows = scaled.shape[0] - 16
    blocks = lax.all_gather(scaled[: n_rows + 8].astype(jnp.float16), "z", axis=0)
    levels = jnp.max(blocks[:, n_rows:].astype(jnp.float32), axis=(1, 2), keepdims=True)
    back = sum(jnp.where(levels == i, 2.0 ** (-17 - 15 * i), 0.0) for i in range(LEVELS))
    split = GROUP * HEAD_DIM

    def columns(first, last):
        part = blocks[:, :n_rows, first:last].astype(jnp.float32) * back
        return part.astype(jnp.bfloat16).reshape(-1, last - first)

    return columns(0, 256), columns(256, split), columns(split, scaled.shape[1])


def project_kv_body(step, weight_ref, tokens_ref, out_ref, held_ref, sem):
    count, size, depth = held_ref.shape
    copies = []
    for k in range(depth // step):
        at = pl.ds(k * step, step)
        copies.append(pltpu.make_async_copy(tokens_ref.at[:, :, at], held_ref.at[:, :, at], sem.at[k]))
        copies[-1].start()
    for k, copy in enumerate(copies):
        copy.wait()
        at = slice(k * step, (k + 1) * step)
        rows = held_ref[:, :, at].reshape(count * size, step)
        product = jnp.dot(rows, weight_ref[at, :], preferred_element_type=jnp.float32)
        if k == 0:
            out_ref[...] = product
        else:
            out_ref[...] += product


def project_q_body(step, first_ref, second_ref, tokens_ref, out_ref):
    count, size, depth = tokens_ref.shape
    split = first_ref.shape[1]
    for k in range(depth // step):
        at = slice(k * step, (k + 1) * step)
        rows = tokens_ref[:, :, at].reshape(count * size, step)
        for to, ref in ((slice(0, split), first_ref), (slice(split, out_ref.shape[1]), second_ref)):
            product = jnp.dot(rows, ref[at, :], preferred_element_type=jnp.float32)
            if k == 0:
                out_ref[:, to] = product
            else:
                out_ref[:, to] += product


def by_core(out):
    first = lax.axis_index("core") == 0
    low, high = out[: out.shape[0] // 2], out[out.shape[0] // 2 :]
    return jnp.where(first, low, high), jnp.where(first, high, low)


def project_kv(weight, tokens):
    depth, columns = weight.shape
    n_rows = tokens.shape[0] * tokens.shape[1]
    step = 768
    out, held = pl.pallas_call(
        functools.partial(project_kv_body, step),
        out_shape=(
            jax.ShapeDtypeStruct((n_rows, columns), jnp.float32),
            jax.ShapeDtypeStruct(tokens.shape, tokens.dtype),
        ),
        in_specs=[vmem(1)[0], pl.BlockSpec(memory_space=pltpu.HBM)],
        out_specs=tuple(vmem(2)),
        scratch_shapes=[pltpu.SemaphoreType.DMA((depth // step,))],
        compiler_params=pltpu.CompilerParams(vmem_limit_bytes=6 * 1024 * 1024),
        cost_estimate=pl.CostEstimate(
            flops=2 * n_rows * depth * columns, bytes_accessed=2 * depth * (columns + n_rows), transcendentals=0
        ),
        name="project_kv",
    )(weight, tokens)
    return *by_core(out), held


def project_q(weights, tokens):
    n_rows = tokens.shape[0] * tokens.shape[1]
    out = pl.pallas_call(
        functools.partial(project_q_body, 1536),
        out_shape=jax.ShapeDtypeStruct((n_rows, sum(weight.shape[1] for weight in weights)), jnp.float32),
        in_specs=vmem(3),
        out_specs=vmem(1)[0],
        compiler_params=pltpu.CompilerParams(vmem_limit_bytes=6 * 1024 * 1024),
        cost_estimate=pl.CostEstimate(flops=10**7, bytes_accessed=10**5, transcendentals=0),
        name="project_q",
    )(*weights, tokens)
    return by_core(out)


def over_keys(left, right):
    return lax.dot_general(left, right, (((0,), (0,)), ((), ())), preferred_element_type=jnp.float32)


def over_features(left, right):
    return lax.dot_general(left, right, (((1,), (1,)), ((), ())), preferred_element_type=jnp.float32)


def window_body(far_ref, near_ref, own_ref, out_ref):
    rows = own_ref.shape[0]
    for i, ref in enumerate((far_ref, near_ref, own_ref)):
        out_ref[i * rows : (i + 1) * rows, :] = ref[...]


def window(far_kv, near_kv, own_kv):
    rows, columns = own_kv.shape
    return pl.pallas_call(
        window_body,
        out_shape=jax.ShapeDtypeStruct((3 * rows, columns), own_kv.dtype),
        in_specs=vmem(3),
        out_specs=vmem(1)[0],
        compiler_params=pltpu.CompilerParams(vmem_limit_bytes=4 * 1024 * 1024),
        cost_estimate=pl.CostEstimate(flops=10**10, bytes_accessed=4 * 10**7, transcendentals=0),
        name="window",
    )(far_kv, near_kv, own_kv)


def attend_body(
    q_part_ref, other_q_ref, window_ref, grad_ref, docs_ref, out_ref, dq_ref, far_out, near_out, own_out, q_ref, k_docs, dk, dv
):
    rows = q_ref.shape[0]
    size = HEAD_DIM
    count = rows // size
    x_hi, z, core = (lax.axis_index(name) for name in CTX)
    block = (x_hi * SIZES["z"] + z) * SIZES["core"] + core
    for i in range(3 * count):
        at = (block - 2) * count + i
        docs = docs_ref[pl.ds(jnp.maximum(at, 0), 1), :].astype(jnp.float32)
        docs = jnp.where(at >= 0, docs, -1.0)
        k_docs[i * size : (i + 1) * size, :] = jnp.transpose(jnp.broadcast_to(docs, (size, size)))
    q_ref[...] = (q_part_ref[...] + other_q_ref[...]).astype(q_ref.dtype)
    scale = HEAD_DIM ** (-0.5)
    dk[...] = jnp.zeros_like(dk)
    dv[...] = jnp.zeros_like(dv)

    def window(which, r):
        return window_ref[r * size : (r + 1) * size + 2 * rows, which * HEAD_DIM : (which + 1) * HEAD_DIM]

    def by_head(ref, r):
        at = slice(r * size, (r + 1) * size)
        return jnp.concatenate([ref[at, h * HEAD_DIM : (h + 1) * HEAD_DIM] for h in range(GROUP)], axis=0)

    for r in range(count):
        first = r * size
        span = 2 * rows + size
        keys, values = window(0, r), window(1, r)
        query, grads = by_head(q_ref, r), by_head(grad_ref, r)
        gap = (
            2 * rows
            + lax.broadcasted_iota(jnp.int32, (span, size), 1)
            - lax.broadcasted_iota(jnp.int32, (span, size), 0)
        )
        same = k_docs[first : first + span, :] == docs_ref[pl.ds(block * count + r, 1), :].astype(jnp.float32)
        allowed = (gap >= 0) & (gap < 2 * rows) & same
        hidden = jnp.where(allowed, jnp.float32(0), jnp.float32(-1e30))
        hidden = jnp.concatenate([hidden] * GROUP, axis=1)
        scores = over_features(keys, query) * scale + hidden
        expo = jnp.exp(scores)
        prob = expo * (1.0 / jnp.sum(expo, axis=0, keepdims=True))
        prob_b = prob.astype(jnp.bfloat16)
        out_t = over_keys(values, prob_b).astype(jnp.bfloat16)
        grads_t = jnp.transpose(grads.astype(jnp.float32))
        delta = jnp.sum(grads_t * out_t.astype(jnp.float32), axis=0, keepdims=True)
        dprob = over_features(values, grads)
        dscore = (prob * (dprob - delta)).astype(jnp.bfloat16)
        to = slice(first, first + span)
        dv[to, :] += jnp.dot(prob_b, grads, preferred_element_type=jnp.float32)
        dk[to, :] += jnp.dot(dscore, query, preferred_element_type=jnp.float32)
        dq = jnp.transpose(over_keys(keys, dscore)) * scale
        out = jnp.transpose(out_t.astype(jnp.float32))
        for h in range(GROUP):
            at = slice(h * size, (h + 1) * size)
            out_ref[first : first + size, at] = out[at, :].astype(out_ref.dtype)
            dq_ref[first : first + size, at] = dq[at, :].astype(dq_ref.dtype)
    for which, terms, factor in ((0, dk, scale), (1, dv, 1.0)):
        at = slice(which * HEAD_DIM, (which + 1) * HEAD_DIM)
        far_out[:, at] = (terms[:rows, :] * factor).astype(far_out.dtype)
        near_out[:, at] = (terms[rows : 2 * rows, :] * factor).astype(near_out.dtype)
        own_out[:, at] = terms[2 * rows :, :] * factor


def attend(q_part, other_q, window_kv, out_grad, docs):
    rows = q_part.shape[0]
    kv_shape = (rows, 2 * HEAD_DIM)
    work = 2 * 3 * rows * 7 * rows // 3 * HEAD_DIM
    return pl.pallas_call(
        attend_body,
        out_shape=(
            jax.ShapeDtypeStruct(q_part.shape, jnp.bfloat16),
            jax.ShapeDtypeStruct(q_part.shape, jnp.bfloat16),
            jax.ShapeDtypeStruct(kv_shape, jnp.bfloat16),
            jax.ShapeDtypeStruct(kv_shape, jnp.bfloat16),
            jax.ShapeDtypeStruct(kv_shape, jnp.float32),
        ),
        in_specs=vmem(5),
        out_specs=tuple(vmem(5)),
        scratch_shapes=[
            pltpu.VMEM(q_part.shape, jnp.bfloat16),
            pltpu.VMEM((3 * rows, HEAD_DIM), jnp.float32),
            pltpu.VMEM((3 * rows, HEAD_DIM), jnp.float32),
            pltpu.VMEM((3 * rows, HEAD_DIM), jnp.float32),
        ],
        compiler_params=pltpu.CompilerParams(vmem_limit_bytes=14 * 1024 * 1024),
        cost_estimate=pl.CostEstimate(flops=5 * work, bytes_accessed=10 * rows * rows, transcendentals=7 * rows * rows),
        name="attend",
    )(q_part, other_q, window_kv, out_grad, docs)


def add_body(dq_ref, own_ref, near_ref, far_ref, out_ref):
    split = dq_ref.shape[1]
    out_ref[:, :split] = dq_ref[...]
    total = own_ref[...] + near_ref[...].astype(jnp.float32) + far_ref[...].astype(jnp.float32)
    out_ref[:, split:] = total.astype(out_ref.dtype)


def add_terms(dq, own, near, far):
    rows, columns = dq.shape
    return pl.pallas_call(
        add_body,
        out_shape=jax.ShapeDtypeStruct((rows, columns + own.shape[1]), jnp.bfloat16),
        in_specs=vmem(4),
        out_specs=vmem(1)[0],
        compiler_params=pltpu.CompilerParams(vmem_limit_bytes=4 * 1024 * 1024),
        name="add_terms",
    )(dq, own, near, far)


def per_device(hidden_in, norm_gain, qkv_weight, out_grad, doc_ids):
    rows = out_grad.shape[0]
    same, flipped = pair_rows(qkv_weight)
    copies = norm_copies(hidden_in, norm_gain)
    same, flipped, copies = lax.optimization_barrier((same, flipped, copies))
    tokens = lax.all_to_all(copies, ("core", *HEAD), split_axis=0, concat_axis=0)
    *q_weight, kv_weight = lax.optimization_barrier(gather_weight(scaled_rows(same, flipped)))
    kv_part, other_kv, tokens = project_kv(kv_weight, tokens)
    own_kv = (kv_part + turned(other_kv, "core", 1)).astype(jnp.bfloat16)
    own_kv, tokens = lax.optimization_barrier((own_kv, tokens))
    q_part, other_q = project_q(q_weight, tokens)
    other_q = turned(other_q, "core", 1)
    near_kv = passed_along(own_kv, 1)
    far_kv = passed_along(own_kv, 2)
    attn_out, dq, far, near, own = attend(q_part, other_q, window(far_kv, near_kv, own_kv), out_grad, doc_ids.reshape(-1, HEAD_DIM))
    from_near = passed_along(near, -1)
    from_far = passed_along(far, -2)
    block = add_terms(dq, own, from_near, from_far)
    return (attn_out, lax.all_to_all(block, HEAD, split_axis=0, concat_axis=1, tiled=True))


def solution(mesh):
    fine = Mesh(mesh.devices.reshape(tuple(SIZES.values())), tuple(SIZES))
    in_specs = (P((*CTX, *HEAD), None), P(), P(CTX, HEAD), P(CTX, HEAD), P())
    out_specs = (P(CTX, HEAD), P((*CTX, *HEAD), None))
    return jax.shard_map(
        per_device, mesh=fine, in_specs=in_specs, out_specs=out_specs, check_vma=False
    )
```

```python
import functools

import jax
import jax.numpy as jnp
from jax import lax
from jax.experimental import pallas as pl
from jax.experimental.pallas import tpu as pltpu
from jax.sharding import Mesh
from jax.sharding import PartitionSpec as P

HEAD_DIM = 128
GROUP = 3
CTX = ("x_hi", "z", "core")
HEAD = ("y", "x_lo")
LEVELS = 8
SIZES = {"x_hi": 2, "z": 16, "core": 2, "y": 4, "x_lo": 2}


def turned(value, axis, steps):
    count = SIZES[axis]
    return lax.ppermute(value, axis, [(i, (i + steps) % count) for i in range(count)])


def passed_along(value, steps):
    count = 64
    first, last = (max(0, -steps), min(count, count - steps))
    return lax.ppermute(value, CTX, [(i, i + steps) for i in range(first, last)])


def vmem(count):
    return [pl.BlockSpec(memory_space=pltpu.VMEM)] * count


def norm_body(hidden_ref, gain_ref, out_ref, held, sem):
    values = hidden_ref[...].astype(jnp.float32)
    mean_sq = jnp.mean(values * values, axis=-1, keepdims=True)
    held[...] = (values * lax.rsqrt(mean_sq + 1e-06) * gain_ref[...]).astype(held.dtype)
    count, _, width = out_ref.shape
    copies = [
        pltpu.make_async_copy(held.at[:, pl.ds(i // (count // 2) * width, width)], out_ref.at[i], sem.at[i])
        for i in range(count)
    ]
    for copy in copies:
        copy.start()
    for copy in copies:
        copy.wait()


def norm_copies(hidden_in, norm_gain):
    rows, width = hidden_in.shape
    count = SIZES["core"] * SIZES["y"] * SIZES["x_lo"]
    return pl.pallas_call(
        norm_body,
        out_shape=jax.ShapeDtypeStruct((count, rows, width // 2), jnp.bfloat16),
        in_specs=vmem(2),
        out_specs=pl.BlockSpec(memory_space=pltpu.HBM),
        scratch_shapes=[pltpu.VMEM((rows, width), jnp.bfloat16), pltpu.SemaphoreType.DMA((count,))],
        compiler_params=pltpu.CompilerParams(vmem_limit_bytes=60 * 1024 * 1024),
        cost_estimate=pl.CostEstimate(
            flops=10 * rows * width, bytes_accessed=(2 + count) * rows * width, transcendentals=0
        ),
        name="norm",
    )(hidden_in, norm_gain.reshape(1, width))


def pair_rows(own):
    def sent(flip):
        pairs = [(c * 32 + i * 2 + (x ^ flip), x * 32 + i * 2 + c) for x in range(2) for i in range(16) for c in range(2)]
        return lax.ppermute(own, CTX, pairs)

    return sent(1), sent(0)


def scale_body(flipped_ref, same_ref, out_ref):
    first = lax.axis_index("x_hi") == 0
    size = same_ref.shape[0]
    same, flipped = same_ref[...].astype(jnp.float32), flipped_ref[...].astype(jnp.float32)
    top = jnp.maximum(jnp.abs(same), jnp.abs(flipped))
    top = jnp.max(jnp.max(top, axis=0, keepdims=True), axis=1, keepdims=True)
    level, scale = jnp.zeros_like(top), jnp.full_like(top, 2.0**17)
    for i in range(1, LEVELS):
        small = top < 2.0 ** (-1 - 15 * i)
        level = jnp.where(small, float(i), level)
        scale = jnp.where(small, 2.0 ** (17 + 15 * i), scale)
    out_ref[:size, :] = (jnp.where(first, same, flipped) * scale).astype(out_ref.dtype)
    out_ref[size : 2 * size, :] = (jnp.where(first, flipped, same) * scale).astype(out_ref.dtype)
    tail = (out_ref.shape[0] - 2 * size, out_ref.shape[1])
    out_ref[2 * size :, :] = jnp.broadcast_to(level, tail).astype(out_ref.dtype)


def scaled_rows(flipped, same):
    return pl.pallas_call(
        scale_body,
        out_shape=jax.ShapeDtypeStruct((2 * same.shape[0] + 16, same.shape[1]), same.dtype),
        in_specs=vmem(2),
        out_specs=vmem(1)[0],
        compiler_params=pltpu.CompilerParams(vmem_limit_bytes=4 * 1024 * 1024),
        name="scale",
    )(flipped, same)


def gather_weight(scaled):
    n_rows = scaled.shape[0] - 16
    blocks = lax.all_gather(scaled[: n_rows + 8].astype(jnp.float16), "z", axis=0)
    levels = jnp.max(blocks[:, n_rows:].astype(jnp.float32), axis=(1, 2), keepdims=True)
    back = sum(jnp.where(levels == i, 2.0 ** (-17 - 15 * i), 0.0) for i in range(LEVELS))
    split = GROUP * HEAD_DIM

    def columns(first, last):
        part = blocks[:, :n_rows, first:last].astype(jnp.float32) * back
        return part.astype(jnp.bfloat16).reshape(-1, last - first)

    return columns(0, 256), columns(256, split), columns(split, scaled.shape[1])


def project_kv_body(step, weight_ref, tokens_ref, out_ref, held_ref, sem):
    count, size, depth = held_ref.shape
    copies = []
    for k in range(depth // step):
        at = pl.ds(k * step, step)
        copies.append(pltpu.make_async_copy(tokens_ref.at[:, :, at], held_ref.at[:, :, at], sem.at[k]))
        copies[-1].start()
    for k, copy in enumerate(copies):
        copy.wait()
        at = slice(k * step, (k + 1) * step)
        rows = held_ref[:, :, at].reshape(count * size, step)
        product = jnp.dot(rows, weight_ref[at, :], preferred_element_type=jnp.float32)
        if k == 0:
            out_ref[...] = product
        else:
            out_ref[...] += product


def project_q_body(step, first_ref, second_ref, tokens_ref, out_ref):
    count, size, depth = tokens_ref.shape
    split = first_ref.shape[1]
    for k in range(depth // step):
        at = slice(k * step, (k + 1) * step)
        rows = tokens_ref[:, :, at].reshape(count * size, step)
        for to, ref in ((slice(0, split), first_ref), (slice(split, out_ref.shape[1]), second_ref)):
            product = jnp.dot(rows, ref[at, :], preferred_element_type=jnp.float32)
            if k == 0:
                out_ref[:, to] = product
            else:
                out_ref[:, to] += product


def by_core(out):
    first = lax.axis_index("core") == 0
    low, high = out[: out.shape[0] // 2], out[out.shape[0] // 2 :]
    return jnp.where(first, low, high), jnp.where(first, high, low)


def project_kv(weight, tokens):
    depth, columns = weight.shape
    n_rows = tokens.shape[0] * tokens.shape[1]
    step = 512
    out, held = pl.pallas_call(
        functools.partial(project_kv_body, step),
        out_shape=(
            jax.ShapeDtypeStruct((n_rows, columns), jnp.float32),
            jax.ShapeDtypeStruct(tokens.shape, tokens.dtype),
        ),
        in_specs=[vmem(1)[0], pl.BlockSpec(memory_space=pltpu.HBM)],
        out_specs=tuple(vmem(2)),
        scratch_shapes=[pltpu.SemaphoreType.DMA((depth // step,))],
        compiler_params=pltpu.CompilerParams(vmem_limit_bytes=6 * 1024 * 1024),
        cost_estimate=pl.CostEstimate(
            flops=2 * n_rows * depth * columns, bytes_accessed=2 * depth * (columns + n_rows), transcendentals=0
        ),
        name="project_kv",
    )(weight, tokens)
    return *by_core(out), held


def project_q(weights, tokens):
    n_rows = tokens.shape[0] * tokens.shape[1]
    out = pl.pallas_call(
        functools.partial(project_q_body, 1536),
        out_shape=jax.ShapeDtypeStruct((n_rows, sum(weight.shape[1] for weight in weights)), jnp.float32),
        in_specs=vmem(3),
        out_specs=vmem(1)[0],
        compiler_params=pltpu.CompilerParams(vmem_limit_bytes=6 * 1024 * 1024),
        cost_estimate=pl.CostEstimate(flops=10**7, bytes_accessed=10**5, transcendentals=0),
        name="project_q",
    )(*weights, tokens)
    return by_core(out)


def over_keys(left, right):
    return lax.dot_general(left, right, (((0,), (0,)), ((), ())), preferred_element_type=jnp.float32)


def over_features(left, right):
    return lax.dot_general(left, right, (((1,), (1,)), ((), ())), preferred_element_type=jnp.float32)


def window_body(far_ref, near_ref, own_ref, out_ref):
    rows = own_ref.shape[0]
    for i, ref in enumerate((far_ref, near_ref, own_ref)):
        out_ref[i * rows : (i + 1) * rows, :] = ref[...]


def window(far_kv, near_kv, own_kv):
    rows, columns = own_kv.shape
    return pl.pallas_call(
        window_body,
        out_shape=jax.ShapeDtypeStruct((3 * rows, columns), own_kv.dtype),
        in_specs=vmem(3),
        out_specs=vmem(1)[0],
        compiler_params=pltpu.CompilerParams(vmem_limit_bytes=4 * 1024 * 1024),
        cost_estimate=pl.CostEstimate(flops=10**10, bytes_accessed=4 * 10**7, transcendentals=0),
        name="window",
    )(far_kv, near_kv, own_kv)


def attend_body(
    q_part_ref, other_q_ref, window_ref, grad_ref, docs_ref, out_ref, dq_ref, far_out, near_out, own_out, q_ref, k_docs, dk, dv
):
    rows = q_ref.shape[0]
    size = HEAD_DIM
    count = rows // size
    x_hi, z, core = (lax.axis_index(name) for name in CTX)
    block = (x_hi * SIZES["z"] + z) * SIZES["core"] + core
    for i in range(3 * count):
        at = (block - 2) * count + i
        docs = docs_ref[pl.ds(jnp.maximum(at, 0), 1), :].astype(jnp.float32)
        docs = jnp.where(at >= 0, docs, -1.0)
        k_docs[i * size : (i + 1) * size, :] = jnp.transpose(jnp.broadcast_to(docs, (size, size)))
    q_ref[...] = (q_part_ref[...] + other_q_ref[...]).astype(q_ref.dtype)
    scale = HEAD_DIM ** (-0.5)
    dk[...] = jnp.zeros_like(dk)
    dv[...] = jnp.zeros_like(dv)

    def window(which, r):
        return window_ref[r * size : (r + 1) * size + 2 * rows, which * HEAD_DIM : (which + 1) * HEAD_DIM]

    def by_head(ref, r):
        at = slice(r * size, (r + 1) * size)
        return jnp.concatenate([ref[at, h * HEAD_DIM : (h + 1) * HEAD_DIM] for h in range(GROUP)], axis=0)

    for r in range(count):
        first = r * size
        span = 2 * rows + size
        keys, values = window(0, r), window(1, r)
        query, grads = by_head(q_ref, r), by_head(grad_ref, r)
        gap = (
            2 * rows
            + lax.broadcasted_iota(jnp.int32, (span, size), 1)
            - lax.broadcasted_iota(jnp.int32, (span, size), 0)
        )
        same = k_docs[first : first + span, :] == docs_ref[pl.ds(block * count + r, 1), :].astype(jnp.float32)
        allowed = (gap >= 0) & (gap < 2 * rows) & same
        hidden = jnp.where(allowed, jnp.float32(0), jnp.float32(-1e30))
        hidden = jnp.concatenate([hidden] * GROUP, axis=1)
        scores = over_features(keys, query) * scale + hidden
        expo = jnp.exp(scores)
        prob = expo * (1.0 / jnp.sum(expo, axis=0, keepdims=True))
        prob_b = prob.astype(jnp.bfloat16)
        out_t = over_keys(values, prob_b).astype(jnp.bfloat16)
        grads_t = jnp.transpose(grads.astype(jnp.float32))
        delta = jnp.sum(grads_t * out_t.astype(jnp.float32), axis=0, keepdims=True)
        dprob = over_features(values, grads)
        dscore = (prob * (dprob - delta)).astype(jnp.bfloat16)
        to = slice(first, first + span)
        dv[to, :] += jnp.dot(prob_b, grads, preferred_element_type=jnp.float32)
        dk[to, :] += jnp.dot(dscore, query, preferred_element_type=jnp.float32)
        dq = jnp.transpose(over_keys(keys, dscore)) * scale
        out = jnp.transpose(out_t.astype(jnp.float32))
        for h in range(GROUP):
            at = slice(h * size, (h + 1) * size)
            out_ref[first : first + size, at] = out[at, :].astype(out_ref.dtype)
            dq_ref[first : first + size, at] = dq[at, :].astype(dq_ref.dtype)
    for which, terms, factor in ((0, dk, scale), (1, dv, 1.0)):
        at = slice(which * HEAD_DIM, (which + 1) * HEAD_DIM)
        far_out[:, at] = (terms[:rows, :] * factor).astype(far_out.dtype)
        near_out[:, at] = (terms[rows : 2 * rows, :] * factor).astype(near_out.dtype)
        own_out[:, at] = terms[2 * rows :, :] * factor


def attend(q_part, other_q, window_kv, out_grad, docs):
    rows = q_part.shape[0]
    kv_shape = (rows, 2 * HEAD_DIM)
    work = 2 * 3 * rows * 7 * rows // 3 * HEAD_DIM
    return pl.pallas_call(
        attend_body,
        out_shape=(
            jax.ShapeDtypeStruct(q_part.shape, jnp.bfloat16),
            jax.ShapeDtypeStruct(q_part.shape, jnp.bfloat16),
            jax.ShapeDtypeStruct(kv_shape, jnp.bfloat16),
            jax.ShapeDtypeStruct(kv_shape, jnp.bfloat16),
            jax.ShapeDtypeStruct(kv_shape, jnp.float32),
        ),
        in_specs=vmem(5),
        out_specs=tuple(vmem(5)),
        scratch_shapes=[
            pltpu.VMEM(q_part.shape, jnp.bfloat16),
            pltpu.VMEM((3 * rows, HEAD_DIM), jnp.float32),
            pltpu.VMEM((3 * rows, HEAD_DIM), jnp.float32),
            pltpu.VMEM((3 * rows, HEAD_DIM), jnp.float32),
        ],
        compiler_params=pltpu.CompilerParams(vmem_limit_bytes=14 * 1024 * 1024),
        cost_estimate=pl.CostEstimate(flops=5 * work, bytes_accessed=10 * rows * rows, transcendentals=7 * rows * rows),
        name="attend",
    )(q_part, other_q, window_kv, out_grad, docs)


def add_body(dq_ref, own_ref, near_ref, far_ref, out_ref):
    split = dq_ref.shape[1]
    out_ref[:, :split] = dq_ref[...]
    total = own_ref[...] + near_ref[...].astype(jnp.float32) + far_ref[...].astype(jnp.float32)
    out_ref[:, split:] = total.astype(out_ref.dtype)


def add_terms(dq, own, near, far):
    rows, columns = dq.shape
    return pl.pallas_call(
        add_body,
        out_shape=jax.ShapeDtypeStruct((rows, columns + own.shape[1]), jnp.bfloat16),
        in_specs=vmem(4),
        out_specs=vmem(1)[0],
        compiler_params=pltpu.CompilerParams(vmem_limit_bytes=4 * 1024 * 1024),
        name="add_terms",
    )(dq, own, near, far)


def place_body(blocks_ref, out_ref):
    count, _, width = blocks_ref.shape
    for j in range(count):
        out_ref[:, j * width : (j + 1) * width] = blocks_ref[j]


def placed(blocks):
    count, rows, width = blocks.shape
    return pl.pallas_call(
        place_body,
        out_shape=jax.ShapeDtypeStruct((rows, count * width), blocks.dtype),
        in_specs=vmem(1),
        out_specs=vmem(1)[0],
        compiler_params=pltpu.CompilerParams(vmem_limit_bytes=2 * 1024 * 1024),
        name="place",
    )(blocks)


def per_device(hidden_in, norm_gain, qkv_weight, out_grad, doc_ids):
    rows = out_grad.shape[0]
    flipped, same = pair_rows(qkv_weight)
    copies = norm_copies(hidden_in, norm_gain)
    flipped, same, copies = lax.optimization_barrier((flipped, same, copies))
    tokens = lax.all_to_all(copies, ("core", *HEAD), split_axis=0, concat_axis=0)
    *q_weight, kv_weight = lax.optimization_barrier(gather_weight(scaled_rows(flipped, same)))
    kv_part, other_kv, tokens = project_kv(kv_weight, tokens)
    own_kv = (kv_part + turned(other_kv, "core", 1)).astype(jnp.bfloat16)
    own_kv, tokens = lax.optimization_barrier((own_kv, tokens))
    q_part, other_q = project_q(q_weight, tokens)
    other_q = turned(other_q, "core", 1)
    near_kv = passed_along(own_kv, 1)
    far_kv = passed_along(own_kv, 2)
    attn_out, dq, far, near, own = attend(q_part, other_q, window(far_kv, near_kv, own_kv), out_grad, doc_ids.reshape(-1, HEAD_DIM))
    from_far = passed_along(far, -2)
    from_near = passed_along(near, -1)
    block = add_terms(dq, own, from_near, from_far)
    count = SIZES["y"] * SIZES["x_lo"]
    block = block.reshape(count, rows // count, block.shape[1])
    return (attn_out, placed(lax.all_to_all(block, HEAD, split_axis=0, concat_axis=0)))


def solution(mesh):
    fine = Mesh(mesh.devices.reshape(tuple(SIZES.values())), tuple(SIZES))
    in_specs = (P((*CTX, *HEAD), None), P(), P(CTX, HEAD), P(CTX, HEAD), P())
    out_specs = (P(CTX, HEAD), P((*CTX, *HEAD), None))
    return jax.shard_map(
        per_device, mesh=fine, in_specs=in_specs, out_specs=out_specs, check_vma=False
    )
```
